512 devices in a mesh: own: 64 (over z, x), pair: 8 (over y, core).
Axes of the slice: x: 4, y: 4, z: 16, core: 2. Of those that a mesh axis runs over, the one named last changes fastest.
Arguments:
- points: bfloat16 [65536, 64], P(('own', 'pair')), may hold values from -6 to 6
- inv_scale: float32 [64], replicated, may hold values from 0.05 to 0.6
- tasks: int32 [65536], P(('own', 'pair')), may hold values from 0 to 7
- task_cov: float32 [8, 8], replicated, may hold values from -0.12 to 1.5, as said below
- solution: float32 [65536, 16], P(('own', 'pair')), may hold values from -6 to 6
- residual: float32 [65536, 16], P(('own', 'pair')), may hold values from -30 to 30
- direction: float32 [65536, 16], P(('own', 'pair')), may hold values from -30 to 30
Outputs:
- new_solution: float32 [65536, 16], P(('own', 'pair'))
- new_residual: float32 [65536, 16], P(('own', 'pair'))
- new_direction: float32 [65536, 16], P(('own', 'pair'))
The draws below stay inside these ranges and needn't reach their ends.
Inputs may be any that keep to these rules, and one draw needn't show every extreme that they name: `task_cov`: symmetric, and each diagonal entry exceeds the sum of magnitudes of the other entries of its row.
All inputs are finite; a program needn't handle non-finite values.
Results may differ from the reference program's by a relative error of at most 0.0044.
Values may be sent and summed in bfloat16 or wider, within the bound.
No kernel may reach another device: no remote copies, remote signals or barrier semaphores. Data moves between devices by JAX's collectives and lax.ppermute only.
A program may use at most 128 MiB of HBM per device.

```python
import math
import jax
import jax.numpy as jnp
from jax import lax

FEATS = 64
PROBES = 16
TASKS = 8
PTS_DEV = 128
POINTS = 65536
N_PAIR = 8


def scaled_rows(key, spread):
    first, second = jax.random.split(key, 2)
    rows = jnp.exp(jax.random.uniform(first, (POINTS, 1), jnp.float32, 0.0, math.log(spread)))
    ramp = jnp.exp(math.log(3.0) * jnp.arange(POINTS).astype(jnp.float32) / POINTS)[:, None]
    values = jnp.clip(jax.random.normal(second, (POINTS, PROBES), jnp.float32), -6.0, 6.0)
    return values * rows * ramp / 6.0


def draw_residual(key, part):
    key = jax.random.fold_in(key, 11)
    return scaled_rows(key, 10.0)


def draw_direction(key, part):
    key = jax.random.fold_in(key, 23)
    return scaled_rows(key, 10.0)


def draw_task_cov(key, part):
    key = jax.random.fold_in(key, 37)
    first, second = jax.random.split(key)
    upper = jax.random.uniform(first, (TASKS, TASKS), jnp.float32, -0.12, 0.12)
    sym = jnp.triu(upper, 1) + jnp.triu(upper, 1).T
    diag = jax.random.uniform(second, (TASKS,), jnp.float32, 1.0, 1.5)
    return sym + jnp.diag(diag)


def touch_ends(result, rng, smallest, top_value):
    index_at = [jax.random.randint(jax.random.fold_in(rng, axis), (), 0, length) for axis, length in enumerate(result.shape)]
    longest = result.shape.index(max(result.shape))
    beside = index_at[:longest] + [(index_at[longest] + 1) % result.shape[longest]] + index_at[longest + 1:]
    return result.at[tuple(index_at)].set(smallest).at[tuple(beside)].set(top_value)


def block_levels(rng, shape, pieces, least, top_value):
    gain = 1.0
    for dim, shards_of in pieces:
        heights = jax.random.uniform(jax.random.fold_in(jax.random.fold_in(rng, 6), dim), (shards_of,), jnp.float32, least / len(pieces), top_value / len(pieces))
        gain = gain * jnp.repeat(jnp.exp(heights), shape[dim] // shards_of).reshape((-1,) + (1,) * (len(shape) - 1 - dim))
    return gain


def normal_values(rng, dims, scale, most, pieces=(), dtype=jnp.bfloat16):
    gain = block_levels(rng, dims, pieces, -0.22, 0.18) if pieces else 1.0
    result = jax.random.normal(rng, dims, jnp.float32) * scale * gain
    return jnp.minimum(jnp.maximum(result, -most), most).astype(dtype)


def setup_inputs(seed: int = 0) -> dict:
    key_of = jax.random.split(jax.random.key(seed), 8)
    points = normal_values(key_of[0], (POINTS, FEATS), 1.0, 6.0, ((0, 512),))
    inv_scale = jnp.clip(jnp.exp(jax.random.uniform(key_of[1], (FEATS,), jnp.float32, math.log(0.05), math.log(0.6))), 0.05, 0.6)
    tasks = touch_ends(jax.random.randint(key_of[2], (POINTS,), 0, TASKS), jax.random.fold_in(key_of[2], 1), 0, TASKS - 1).astype(jnp.int32)
    task_cov = draw_task_cov(jax.random.fold_in(key_of[7], 71), 0)
    solution = normal_values(key_of[4], (POINTS, PROBES), 1.0, 6.0, ((0, 512),), jnp.float32)
    residual = draw_residual(jax.random.fold_in(key_of[7], 71), 0)
    direction = draw_direction(jax.random.fold_in(key_of[7], 71), 0)
    return dict(points=points, inv_scale=inv_scale, tasks=tasks, task_cov=task_cov, solution=solution, residual=residual, direction=direction)


noise_var = 1.0


def reference(points, inv_scale, tasks, task_cov, solution, residual, direction):
    scaled = (points.astype(jnp.float32) * inv_scale).astype(jnp.bfloat16)
    sqnorm = jnp.sum(jnp.square(scaled.astype(jnp.float32)), axis=1)
    labels = jnp.arange(TASKS).astype(jnp.int32)
    onehot = (tasks[:, None] == labels[None, :]).astype(jnp.float32)
    cov_rows = jnp.dot(onehot, task_cov, precision=lax.Precision.HIGHEST)
    dir_low = direction.astype(jnp.bfloat16)
    group = PTS_DEV * N_PAIR
    blocks = POINTS // group
    scaled_b = scaled.reshape(blocks, group, FEATS)
    sq_b = sqnorm.reshape(blocks, group)
    onehot_b = onehot.reshape(blocks, group, TASKS)
    cov_b = cov_rows.reshape(blocks, group, TASKS)
    dir_b = dir_low.reshape(blocks, group, PROBES)

    def row_block(inputs):
        row_scaled, row_sq, row_cov = inputs

        def add_block(total, cols):
            col_scaled, col_sq, col_hot, col_dir = cols
            inner_prod = jnp.dot(row_scaled, col_scaled.T, preferred_element_type=jnp.float32)
            factor = jnp.dot(row_cov, col_hot.T, precision=lax.Precision.HIGHEST)
            kernel = (factor * jnp.exp(-0.5 * (row_sq[:, None] + col_sq[None, :] - 2.0 * inner_prod))).astype(jnp.bfloat16)
            return total + jnp.dot(kernel, col_dir, preferred_element_type=jnp.float32), None

        start = jnp.zeros((group, PROBES), jnp.float32)
        total, unused = lax.scan(add_block, start, (scaled_b, sq_b, onehot_b, dir_b))
        return total

    kernel_prod = lax.map(row_block, (scaled_b, sq_b, cov_b)).reshape(POINTS, PROBES)
    product = kernel_prod + noise_var * direction
    curvature = jnp.sum(direction * product, axis=0)
    norm_old = jnp.sum(residual * residual, axis=0)
    step_size = norm_old / curvature
    new_solution = solution + step_size * direction
    new_residual = residual - step_size * product
    norm_new = jnp.sum(new_residual * new_residual, axis=0)
    new_direction = new_residual + (norm_new / norm_old) * direction
    return new_solution, new_residual, new_direction
```

```python
import math

import jax
import jax.numpy as jnp
from jax import lax
from jax.experimental import pallas as pl
from jax.experimental.pallas import tpu as pltpu
from jax.sharding import Mesh
from jax.sharding import PartitionSpec as P

noise_var = 1.0
log2e = math.log2(math.e)
f32, bf16 = jnp.float32, jnp.bfloat16

FEATS, PROBES, LEVELS, LANES = 64, 16, 8, 128
TASK_AT, DIR_AT = FEATS, FEATS + 8
ROW_ROWS, COL_ROWS = DIR_AT, DIR_AT + PROBES
TAIL = 16
DEPTH = 3 * FEATS + TAIL
TILE = 512

SHAPE = (16, 4, 4, 2)
AXES = ("z", "x", "y", "core")
LINE, PLANE = "z", ("x", "y", "core")


def split3(value):
    high = value.astype(bf16)
    rest = value - high.astype(f32)
    mid = rest.astype(bf16)
    return high, mid, (rest - mid.astype(f32)).astype(bf16)


def tail_rows(norm, first):
    high, mid, low = split3(norm)
    row = lax.broadcasted_iota(jnp.int32, (TAIL, norm.shape[1]), 0)
    value = jnp.where(row == first, high.astype(f32), 0.0)
    value = jnp.where(row == first + 1, mid.astype(f32), value)
    value = jnp.where(row == first + 2, low.astype(f32), value)
    ones_at = 3 - first
    return jnp.where((row >= ones_at) & (row < ones_at + 3), 1.0, value).astype(bf16)


def pack_kernel(points_ref, scale_ref, tasks_ref, dir_ref, rows_ref, cols_ref):
    scaled = (points_ref[...].astype(f32) * scale_ref[...]).astype(bf16)
    turned = scaled.astype(f32).T
    task = jnp.broadcast_to(tasks_ref[...].astype(f32), (8, LANES))
    shared = jnp.concatenate([turned, task], axis=0).astype(bf16)
    whole = jnp.concatenate([turned, task, dir_ref[...]], axis=0).astype(bf16)
    for k in range(rows_ref.shape[0]):
        rows_ref[k] = shared
    for k in range(cols_ref.shape[0]):
        cols_ref[k] = whole


def block_kernel(rows_ref, cols_ref, cov_ref, out_ref, row_mat, col_mat, dir_mat):
    n_rows, n_cols = rows_ref.shape[0], cols_ref.shape[0]
    for k in range(n_rows):
        at = pl.ds(k * LANES, LANES)
        scaled = rows_ref[k, :FEATS, :]
        wide = scaled.astype(f32)
        norm = jnp.sum(wide * wide, axis=0, keepdims=True) * (-0.5 * log2e)
        for part in range(3):
            row_mat[part * FEATS : (part + 1) * FEATS, at] = scaled
        row_mat[3 * FEATS :, at] = tail_rows(norm, 3)
    for k in range(n_cols):
        at = pl.ds(k * LANES, LANES)
        wide = cols_ref[k, :FEATS, :].astype(f32)
        norm = jnp.sum(wide * wide, axis=0, keepdims=True) * (-0.5 * log2e)
        high, mid, low = split3(wide * log2e)
        stack = jnp.concatenate([high, mid, low, tail_rows(norm, 0)], axis=0)
        col_mat[at, :] = stack.astype(f32).T.astype(bf16)
        task = cols_ref[k, TASK_AT:DIR_AT, :][0:1].astype(f32)
        dirs = cols_ref[k, DIR_AT:, :].astype(f32)
        dir_mat[:, at] = jnp.concatenate(
            [jnp.where(task == float(level), dirs, 0.0) for level in range(LEVELS)], axis=0
        ).astype(bf16)

    def step(tile, carry):
        base = pl.multiple_of(tile * TILE, TILE)
        exponent = jnp.dot(
            col_mat[...], row_mat[:, pl.ds(base, TILE)], preferred_element_type=f32
        )
        kernel = jnp.exp2(exponent).astype(bf16)
        sums = jnp.dot(dir_mat[...], kernel, preferred_element_type=f32)
        for j in range(TILE // LANES):
            k = tile * (TILE // LANES) + j
            task = rows_ref[k, TASK_AT:DIR_AT, :][0:1].astype(f32)
            cov = jnp.zeros((LEVELS, LANES), f32)
            for level in range(LEVELS):
                cov = cov + jnp.where(task == float(level), cov_ref[:, level : level + 1], 0.0)
            total = jnp.zeros((PROBES, LANES), f32)
            for level in range(LEVELS):
                part = sums[level * PROBES : (level + 1) * PROBES, j * LANES : (j + 1) * LANES]
                total = total + cov[level : level + 1, :] * part
            out_ref[k] = total
        return carry

    lax.fori_loop(0, n_rows * LANES // TILE, step, 0)


def product_kernel(parts_ref, dir_ref, res_ref, product_ref, stats_ref):
    direction, residual = dir_ref[...], res_ref[...]
    product = jnp.sum(parts_ref[...], axis=0) + noise_var * direction
    product_ref[...] = product
    terms = jnp.concatenate(
        [direction * product, residual * residual, residual * product, product * product], axis=0
    )
    sums = jnp.sum(terms.T, axis=0, keepdims=True)
    row = jnp.concatenate([sums, jnp.zeros((1, LANES - sums.shape[1]), f32)], axis=1)
    stats_ref[...] = jnp.broadcast_to(row[None], stats_ref.shape)


def call(kernel, out_shape, n_in, scratch=(), limit=16):
    vmem = pl.BlockSpec(memory_space=pltpu.VMEM)
    many = isinstance(out_shape, (list, tuple))
    return pl.pallas_call(
        kernel,
        out_shape=out_shape,
        in_specs=[vmem] * n_in,
        out_specs=[vmem] * len(out_shape) if many else vmem,
        scratch_shapes=scratch,
        compiler_params=pltpu.CompilerParams(vmem_limit_bytes=limit * 2**20),
    )


def body(points, inv_scale, tasks, task_cov, solution, residual, direction):
    line, plane = SHAPE[0], math.prod(SHAPE[1:])
    dir_t, res_t, sol_t = direction.T, residual.T, solution.T
    row_send, col_send = call(
        pack_kernel,
        [
            jax.ShapeDtypeStruct((plane, ROW_ROWS, LANES), bf16),
            jax.ShapeDtypeStruct((line, COL_ROWS, LANES), bf16),
        ],
        4,
    )(points, inv_scale[None, :], tasks[None, :], dir_t)
    cols = lax.all_to_all(col_send, LINE, 0, 0)
    rows = lax.all_to_all(row_send, PLANE, 0, 0)
    partial = call(
        block_kernel,
        jax.ShapeDtypeStruct((plane, PROBES, LANES), f32),
        3,
        [
            pltpu.VMEM((DEPTH, plane * LANES), bf16),
            pltpu.VMEM((line * LANES, DEPTH), bf16),
            pltpu.VMEM((LEVELS * PROBES, line * LANES), bf16),
        ],
        limit=40,
    )(rows, cols, task_cov)
    parts = lax.all_to_all(partial, PLANE, 0, 0)
    product, stats = call(
        product_kernel,
        [
            jax.ShapeDtypeStruct((PROBES, LANES), f32),
            jax.ShapeDtypeStruct((plane, 1, LANES), f32),
        ],
        3,
    )(parts, dir_t, res_t)
    stats = jnp.sum(lax.all_to_all(stats, PLANE, 0, 0), axis=0)
    stats = jnp.broadcast_to(stats[None], (line,) + stats.shape)
    stats = jnp.sum(lax.all_to_all(stats, LINE, 0, 0), axis=(0, 1))
    curvature, norm_old, cross, norm_product = (
        stats[k * PROBES : (k + 1) * PROBES][:, None] for k in range(4)
    )
    step_size = norm_old / curvature
    norm_new = norm_old + step_size * (step_size * norm_product - 2.0 * cross)
    new_residual = res_t - step_size * product
    new_solution = sol_t + step_size * dir_t
    new_direction = new_residual + norm_new / norm_old * dir_t
    return (new_solution.T, new_residual.T, new_direction.T)


def solution(mesh):
    fine = Mesh(mesh.devices.reshape(SHAPE), AXES)
    rows, flat = P(AXES, None), P(AXES)
    return jax.shard_map(
        body,
        mesh=fine,
        in_specs=(rows, P(), flat, P(), rows, rows, rows),
        out_specs=(rows, rows, rows),
        check_vma=False,
    )
```

```python
import math

import jax
import jax.numpy as jnp
from jax import lax
from jax.experimental import pallas as pl
from jax.experimental.pallas import tpu as pltpu
from jax.sharding import Mesh
from jax.sharding import PartitionSpec as P

noise_var = 1.0
f32, bf16 = jnp.float32, jnp.bfloat16

FEATS, PROBES, LEVELS, LANES = 64, 16, 8, 128
TASK_AT, DIR_AT = FEATS, FEATS + 8
ROW_ROWS, COL_ROWS = DIR_AT, DIR_AT + PROBES
TAIL = 16
DEPTH = FEATS + TAIL
TILE = 1024

SHAPE = (16, 4, 4, 2)
AXES = ("z", "x", "y", "core")
LINE, PLANE = "z", ("x", "y", "core")


def split3(value):
    high = value.astype(bf16)
    rest = value - high.astype(f32)
    mid = rest.astype(bf16)
    return high, mid, (rest - mid.astype(f32)).astype(bf16)


def tail_rows(norm, first):
    high, mid, low = split3(norm)
    row = lax.broadcasted_iota(jnp.int32, (TAIL, norm.shape[1]), 0)
    value = jnp.where(row == first, high.astype(f32), 0.0)
    value = jnp.where(row == first + 1, mid.astype(f32), value)
    value = jnp.where(row == first + 2, low.astype(f32), value)
    ones_at = 3 - first
    return jnp.where((row >= ones_at) & (row < ones_at + 3), 1.0, value).astype(bf16)


def pack_kernel(points_ref, scale_ref, tasks_ref, dir_ref, rows_ref, cols_ref):
    scale = jnp.broadcast_to(scale_ref[...], (LANES, FEATS)).T
    scaled = points_ref[...].astype(f32) * scale
    task = jnp.broadcast_to(tasks_ref[...].astype(f32), (8, LANES))
    rows_ref[...] = jnp.concatenate([scaled, task], axis=0).astype(bf16)
    whole = jnp.concatenate([scaled, task, dir_ref[...]], axis=0).astype(bf16)
    for k in range(cols_ref.shape[0]):
        cols_ref[k] = whole


def block_kernel(rows_ref, cols_ref, cov_ref, out_ref, row_mat, col_mat, dir_mat):
    n_rows, n_cols = rows_ref.shape[0], cols_ref.shape[0]
    for k in range(n_rows):
        at = pl.ds(k * LANES, LANES)
        scaled = rows_ref[k, :FEATS, :]
        wide = scaled.astype(f32)
        norm = jnp.sum(wide * wide, axis=0, keepdims=True) * -0.5
        row_mat[:FEATS, at] = scaled
        row_mat[FEATS:, at] = tail_rows(norm, 3)
    for k in range(n_cols):
        at = pl.ds(k * LANES, LANES)
        scaled = cols_ref[k, :FEATS, :]
        wide = scaled.astype(f32)
        norm = jnp.sum(wide * wide, axis=0, keepdims=True) * -0.5
        stack = jnp.concatenate([scaled, tail_rows(norm, 0)], axis=0)
        col_mat[at, :] = stack.astype(f32).T.astype(bf16)
        task = cols_ref[k, TASK_AT:DIR_AT, :][0:1].astype(f32)
        dirs = cols_ref[k, DIR_AT:, :].astype(f32)
        dir_mat[:, at] = jnp.concatenate(
            [jnp.where(task == float(level), dirs, 0.0) for level in range(LEVELS)], axis=0
        ).astype(bf16)

    def step(tile, carry):
        base = pl.multiple_of(tile * TILE, TILE)
        exponent = jnp.dot(
            col_mat[...], row_mat[:, pl.ds(base, TILE)], preferred_element_type=f32
        )
        kernel = jnp.exp(exponent).astype(bf16)
        sums = jnp.dot(dir_mat[...], kernel, preferred_element_type=f32)
        for j in range(TILE // LANES):
            k = tile * (TILE // LANES) + j
            task = rows_ref[k, TASK_AT:DIR_AT, :][0:1].astype(f32)
            cov = jnp.zeros((LEVELS, LANES), f32)
            for level in range(LEVELS):
                cov = cov + jnp.where(task == float(level), cov_ref[:, level : level + 1], 0.0)
            total = jnp.zeros((PROBES, LANES), f32)
            for level in range(LEVELS):
                part = sums[level * PROBES : (level + 1) * PROBES, j * LANES : (j + 1) * LANES]
                total = total + cov[level : level + 1, :] * part
            out_ref[k] = total
        return carry

    lax.fori_loop(0, n_rows * LANES // TILE, step, 0)


def product_kernel(parts_ref, dir_ref, res_ref, product_ref, stats_ref):
    direction, residual = dir_ref[...], res_ref[...]
    product = jnp.sum(parts_ref[...], axis=0) + noise_var * direction
    product_ref[...] = product
    terms = jnp.concatenate(
        [direction * product, residual * residual, residual * product, product * product], axis=0
    )
    sums = jnp.sum(terms.T, axis=0, keepdims=True)
    row = jnp.concatenate([sums, jnp.zeros((1, LANES - sums.shape[1]), f32)], axis=1)
    stats_ref[...] = jnp.broadcast_to(row[None], stats_ref.shape)


def update_kernel(stats_ref, product_ref, dir_ref, res_ref, sol_ref, new_sol_ref, new_res_ref, new_dir_ref):
    sums = jnp.broadcast_to(jnp.sum(stats_ref[...], axis=0), (LANES, LANES)).T
    curvature, norm_old, cross, norm_product = (
        sums[k * PROBES : (k + 1) * PROBES] for k in range(4)
    )
    step_size = norm_old / curvature
    norm_new = norm_old + step_size * (step_size * norm_product - 2.0 * cross)
    direction = dir_ref[...]
    new_residual = res_ref[...] - step_size * product_ref[...]
    new_sol_ref[...] = sol_ref[...] + step_size * direction
    new_res_ref[...] = new_residual
    new_dir_ref[...] = new_residual + norm_new / norm_old * direction


def call(kernel, out_shape, n_in, scratch=(), limit=16):
    vmem = pl.BlockSpec(memory_space=pltpu.VMEM)
    many = isinstance(out_shape, (list, tuple))
    return pl.pallas_call(
        kernel,
        out_shape=out_shape,
        in_specs=[vmem] * n_in,
        out_specs=[vmem] * len(out_shape) if many else vmem,
        scratch_shapes=scratch,
        compiler_params=pltpu.CompilerParams(vmem_limit_bytes=limit * 2**20),
    )


def body(points, inv_scale, tasks, task_cov, solution, residual, direction):
    line, plane = SHAPE[0], math.prod(SHAPE[1:])
    dir_t, res_t, sol_t = direction.T, residual.T, solution.T
    row_send, col_send = call(
        pack_kernel,
        [
            jax.ShapeDtypeStruct((ROW_ROWS, LANES), bf16),
            jax.ShapeDtypeStruct((line, COL_ROWS, LANES), bf16),
        ],
        4,
    )(points.T, inv_scale[None, :], tasks[None, :], dir_t)
    cols = lax.all_to_all(col_send, LINE, 0, 0)
    rows = lax.all_gather(row_send, PLANE)
    partial = call(
        block_kernel,
        jax.ShapeDtypeStruct((plane, PROBES, LANES), f32),
        3,
        [
            pltpu.VMEM((DEPTH, plane * LANES), bf16),
            pltpu.VMEM((line * LANES, DEPTH), bf16),
            pltpu.VMEM((LEVELS * PROBES, line * LANES), bf16),
        ],
        limit=40,
    )(rows, cols, task_cov)
    parts = lax.all_to_all(partial, PLANE, 0, 0)
    product, stats = call(
        product_kernel,
        [
            jax.ShapeDtypeStruct((PROBES, LANES), f32),
            jax.ShapeDtypeStruct((plane, 1, LANES), f32),
        ],
        3,
    )(parts, dir_t, res_t)
    stats = jnp.sum(lax.all_to_all(stats, PLANE, 0, 0), axis=0)
    stats = jnp.broadcast_to(stats[None], (line,) + stats.shape)
    stats = lax.all_to_all(stats, LINE, 0, 0)
    like = jax.ShapeDtypeStruct((PROBES, LANES), f32)
    new_solution, new_residual, new_direction = call(update_kernel, [like] * 3, 5)(
        stats, product, dir_t, res_t, sol_t
    )
    return (new_solution.T, new_residual.T, new_direction.T)


def solution(mesh):
    fine = Mesh(mesh.devices.reshape(SHAPE), AXES)
    rows, flat = P(AXES, None), P(AXES)
    return jax.shard_map(
        body,
        mesh=fine,
        in_specs=(rows, P(), flat, P(), rows, rows, rows),
        out_specs=(rows, rows, rows),
        check_vma=False,
    )
```

```python
import math

import jax
import jax.numpy as jnp
from jax import lax
from jax.experimental import pallas as pl
from jax.experimental.pallas import tpu as pltpu
from jax.sharding import Mesh
from jax.sharding import PartitionSpec as P

noise_var = 1.0
f32, bf16 = jnp.float32, jnp.bfloat16

FEATS, PROBES, LEVELS, LANES = 64, 16, 8, 128
TASK_AT, DIR_AT = FEATS, FEATS + 8
ROW_ROWS, COL_ROWS = DIR_AT, DIR_AT + PROBES
TAIL = 16
DEPTH = FEATS + TAIL
TILE = 1024

SHAPE = (16, 4, 4, 2)
AXES = ("z", "x", "y", "core")
LINE, PLANE = "z", ("x", "y", "core")


def split3(value):
    high = value.astype(bf16)
    rest = value - high.astype(f32)
    mid = rest.astype(bf16)
    return high, mid, (rest - mid.astype(f32)).astype(bf16)


def tail_rows(norm, first):
    high, mid, low = split3(norm)
    row = lax.broadcasted_iota(jnp.int32, (TAIL, norm.shape[1]), 0)
    value = jnp.where(row == first, high.astype(f32), 0.0)
    value = jnp.where(row == first + 1, mid.astype(f32), value)
    value = jnp.where(row == first + 2, low.astype(f32), value)
    ones_at = 3 - first
    return jnp.where((row >= ones_at) & (row < ones_at + 3), 1.0, value).astype(bf16)


def pack_kernel(points_ref, scale_ref, tasks_ref, dir_ref, rows_ref, cols_ref):
    scale = jnp.broadcast_to(scale_ref[...], (LANES, FEATS)).T
    scaled = points_ref[...].astype(f32) * scale
    task = jnp.broadcast_to(tasks_ref[...].astype(f32), (8, LANES))
    rows_ref[...] = jnp.concatenate([scaled, task], axis=0).astype(bf16)
    whole = jnp.concatenate([scaled, task, dir_ref[...]], axis=0).astype(bf16)
    for k in range(cols_ref.shape[0]):
        cols_ref[k] = whole


def block_kernel(rows_ref, cols_ref, cov_ref, out_ref, row_mat, col_mat, dir_mat):
    n_rows, n_cols = rows_ref.shape[0], cols_ref.shape[0]
    for k in range(n_rows):
        at = pl.ds(k * LANES, LANES)
        scaled = rows_ref[k, :FEATS, :]
        wide = scaled.astype(f32)
        norm = jnp.sum(wide * wide, axis=0, keepdims=True) * -0.5
        row_mat[:FEATS, at] = scaled
        row_mat[FEATS:, at] = tail_rows(norm, 3)
    for k in range(n_cols):
        at = pl.ds(k * LANES, LANES)
        scaled = cols_ref[k, :FEATS, :]
        wide = scaled.astype(f32)
        norm = jnp.sum(wide * wide, axis=0, keepdims=True) * -0.5
        stack = jnp.concatenate([scaled, tail_rows(norm, 0)], axis=0)
        col_mat[at, :] = stack.astype(f32).T.astype(bf16)
        task = cols_ref[k, TASK_AT:DIR_AT, :][0:1].astype(f32)
        dirs = cols_ref[k, DIR_AT:, :].astype(f32)
        dir_mat[:, at] = jnp.concatenate(
            [jnp.where(task == float(level), dirs, 0.0) for level in range(LEVELS)], axis=0
        ).astype(bf16)

    def step(tile, carry):
        base = pl.multiple_of(tile * TILE, TILE)
        exponent = jnp.dot(
            col_mat[...], row_mat[:, pl.ds(base, TILE)], preferred_element_type=f32
        )
        kernel = jnp.exp(exponent).astype(bf16)
        sums = jnp.dot(dir_mat[...], kernel, preferred_element_type=f32)
        for j in range(TILE // LANES):
            k = tile * (TILE // LANES) + j
            task = rows_ref[k, TASK_AT:DIR_AT, :][0:1].astype(f32)
            cov = jnp.zeros((LEVELS, LANES), f32)
            for level in range(LEVELS):
                cov = cov + jnp.where(task == float(level), cov_ref[:, level : level + 1], 0.0)
            total = jnp.zeros((PROBES, LANES), f32)
            for level in range(LEVELS):
                part = sums[level * PROBES : (level + 1) * PROBES, j * LANES : (j + 1) * LANES]
                total = total + cov[level : level + 1, :] * part
            out_ref[k] = total
        return carry

    lax.fori_loop(0, n_rows * LANES // TILE, step, 0)


def product_kernel(parts_ref, dir_ref, res_ref, product_ref, stats_ref):
    direction, residual = dir_ref[...], res_ref[...]
    product = jnp.sum(parts_ref[...], axis=0) + noise_var * direction
    product_ref[...] = product
    terms = jnp.concatenate(
        [direction * product, residual * residual, residual * product, product * product], axis=0
    )
    sums = jnp.sum(terms.T, axis=0, keepdims=True)
    row = jnp.concatenate([sums, jnp.zeros((1, LANES - sums.shape[1]), f32)], axis=1)
    stats_ref[...] = jnp.broadcast_to(row[None], stats_ref.shape)


def update_kernel(stats_ref, product_ref, dir_ref, res_ref, sol_ref, new_sol_ref, new_res_ref, new_dir_ref):
    sums = jnp.broadcast_to(jnp.sum(stats_ref[...], axis=0), (LANES, LANES)).T
    curvature, norm_old, cross, norm_product = (
        sums[k * PROBES : (k + 1) * PROBES] for k in range(4)
    )
    step_size = norm_old / curvature
    norm_new = norm_old + step_size * (step_size * norm_product - 2.0 * cross)
    direction = dir_ref[...]
    new_residual = res_ref[...] - step_size * product_ref[...]
    new_sol_ref[...] = sol_ref[...] + step_size * direction
    new_res_ref[...] = new_residual
    new_dir_ref[...] = new_residual + norm_new / norm_old * direction


def call(kernel, out_shape, n_in, scratch=(), limit=16):
    vmem = pl.BlockSpec(memory_space=pltpu.VMEM)
    many = isinstance(out_shape, (list, tuple))
    return pl.pallas_call(
        kernel,
        out_shape=out_shape,
        in_specs=[vmem] * n_in,
        out_specs=[vmem] * len(out_shape) if many else vmem,
        scratch_shapes=scratch,
        compiler_params=pltpu.CompilerParams(vmem_limit_bytes=limit * 2**20),
    )


def body(points, inv_scale, tasks, task_cov, solution, residual, direction):
    line, plane = SHAPE[0], math.prod(SHAPE[1:])
    dir_t, res_t, sol_t = direction.T, residual.T, solution.T
    row_send, col_send = call(
        pack_kernel,
        [
            jax.ShapeDtypeStruct((ROW_ROWS, LANES), bf16),
            jax.ShapeDtypeStruct((line, COL_ROWS, LANES), bf16),
        ],
        4,
    )(points.T, inv_scale[None, :], tasks[None, :], dir_t)
    cols = lax.all_to_all(col_send, LINE, 0, 0)
    rows = lax.all_gather(row_send, PLANE)
    partial = call(
        block_kernel,
        jax.ShapeDtypeStruct((plane, PROBES, LANES), f32),
        3,
        [
            pltpu.VMEM((DEPTH, plane * LANES), bf16),
            pltpu.VMEM((line * LANES, DEPTH), bf16),
            pltpu.VMEM((LEVELS * PROBES, line * LANES), bf16),
        ],
        limit=40,
    )(rows, cols, task_cov)
    parts = lax.all_to_all(partial, PLANE, 0, 0)
    product, stats = call(
        product_kernel,
        [
            jax.ShapeDtypeStruct((PROBES, LANES), f32),
            jax.ShapeDtypeStruct((plane, 1, LANES), f32),
        ],
        3,
    )(parts, dir_t, res_t)
    stats = jnp.sum(lax.all_to_all(stats, PLANE, 0, 0), axis=0)
    stats = jnp.broadcast_to(stats[None], (line,) + stats.shape)
    stats = lax.all_to_all(stats, LINE, 0, 0, axis_index_groups=[[(k + 8) % 16 for k in range(16)]])
    like = jax.ShapeDtypeStruct((PROBES, LANES), f32)
    new_solution, new_residual, new_direction = call(update_kernel, [like] * 3, 5)(
        stats, product, dir_t, res_t, sol_t
    )
    return (new_solution.T, new_residual.T, new_direction.T)


def solution(mesh):
    fine = Mesh(mesh.devices.reshape(SHAPE), AXES)
    rows, flat = P(AXES, None), P(AXES)
    return jax.shard_map(
        body,
        mesh=fine,
        in_specs=(rows, P(), flat, P(), rows, rows, rows),
        out_specs=(rows, rows, rows),
        check_vma=False,
    )
```

```python
import math

import jax
import jax.numpy as jnp
from jax import lax
from jax.experimental import pallas as pl
from jax.experimental.pallas import tpu as pltpu
from jax.sharding import Mesh
from jax.sharding import PartitionSpec as P

noise_var = 1.0
f32, bf16 = jnp.float32, jnp.bfloat16

FEATS, PROBES, LEVELS, LANES = 64, 16, 8, 128
TASK_AT, DIR_AT = FEATS, FEATS + 8
ROW_ROWS, COL_ROWS = DIR_AT, DIR_AT + PROBES
TAIL = 16
DEPTH = FEATS + TAIL
TILE = 1024

SHAPE = (16, 4, 4, 2)
AXES = ("z", "x", "y", "core")
LINE, PLANE = "z", ("x", "y", "core")
GATHER_ORDER = [[(k + 12) % SHAPE[0] for k in range(SHAPE[0])]]
SCALAR_ORDER = [[(k + 8) % SHAPE[0] for k in range(SHAPE[0])]]


def split3(value):
    high = value.astype(bf16)
    rest = value - high.astype(f32)
    mid = rest.astype(bf16)
    return high, mid, (rest - mid.astype(f32)).astype(bf16)


def tail_rows(norm, first):
    high, mid, low = split3(norm)
    row = lax.broadcasted_iota(jnp.int32, (TAIL, norm.shape[1]), 0)
    value = jnp.where(row == first, high.astype(f32), 0.0)
    value = jnp.where(row == first + 1, mid.astype(f32), value)
    value = jnp.where(row == first + 2, low.astype(f32), value)
    ones_at = 3 - first
    return jnp.where((row >= ones_at) & (row < ones_at + 3), 1.0, value).astype(bf16)


def pack_kernel(points_in, scale_in, tasks_in, dir_in, rows_ref, cols_ref, points_ref, scale_ref, tasks_ref, dir_ref, sems):
    pairs = ((points_in, points_ref), (scale_in, scale_ref), (tasks_in, tasks_ref), (dir_in, dir_ref))
    copies = [pltpu.make_async_copy(src, dst, sems.at[k]) for k, (src, dst) in enumerate(pairs)]
    for copy in copies:
        copy.start()
    for copy in copies:
        copy.wait()
    scale = jnp.broadcast_to(scale_ref[...], (LANES, FEATS)).T
    scaled = points_ref[...].astype(f32) * scale
    task = jnp.broadcast_to(tasks_ref[...].astype(f32), (8, LANES))
    shared = jnp.concatenate([scaled, task], axis=0).astype(bf16)
    whole = jnp.concatenate([scaled, task, dir_ref[...]], axis=0).astype(bf16)
    rows_ref[...] = shared
    for k in range(cols_ref.shape[0]):
        cols_ref[k] = whole


def block_kernel(rows_ref, cols_ref, cov_ref, out_ref, row_mat, col_mat, dir_mat):
    n_rows, n_cols = rows_ref.shape[0], cols_ref.shape[0]
    for k in range(n_rows):
        at = pl.ds(k * LANES, LANES)
        scaled = rows_ref[k, :FEATS, :]
        wide = scaled.astype(f32)
        norm = jnp.sum(wide * wide, axis=0, keepdims=True) * -0.5
        row_mat[:FEATS, at] = scaled
        row_mat[FEATS:, at] = tail_rows(norm, 3)
    for k in range(n_cols):
        at = pl.ds(k * LANES, LANES)
        scaled = cols_ref[k, :FEATS, :]
        wide = scaled.astype(f32)
        norm = jnp.sum(wide * wide, axis=0, keepdims=True) * -0.5
        stack = jnp.concatenate([scaled, tail_rows(norm, 0)], axis=0)
        col_mat[at, :] = stack.astype(f32).T.astype(bf16)
        task = cols_ref[k, TASK_AT:DIR_AT, :][0:1].astype(f32)
        dirs = cols_ref[k, DIR_AT:, :].astype(f32)
        dir_mat[:, at] = jnp.concatenate(
            [jnp.where(task == float(level), dirs, 0.0) for level in range(LEVELS)], axis=0
        ).astype(bf16)

    def step(tile, carry):
        base = pl.multiple_of(tile * TILE, TILE)
        exponent = jnp.dot(
            col_mat[...], row_mat[:, pl.ds(base, TILE)], preferred_element_type=f32
        )
        kernel = jnp.exp(exponent).astype(bf16)
        sums = jnp.dot(dir_mat[...], kernel, preferred_element_type=f32)
        for j in range(TILE // LANES):
            k = tile * (TILE // LANES) + j
            task = rows_ref[k, TASK_AT:DIR_AT, :][0:1].astype(f32)
            cov = jnp.zeros((LEVELS, LANES), f32)
            for level in range(LEVELS):
                cov = cov + jnp.where(task == float(level), cov_ref[:, level : level + 1], 0.0)
            total = jnp.zeros((PROBES, LANES), f32)
            for level in range(LEVELS):
                part = sums[level * PROBES : (level + 1) * PROBES, j * LANES : (j + 1) * LANES]
                total = total + cov[level : level + 1, :] * part
            out_ref[k] = total
        return carry

    lax.fori_loop(0, n_rows * LANES // TILE, step, 0)


def product_kernel(parts_ref, dir_ref, res_ref, product_ref, stats_ref):
    direction, residual = dir_ref[...], res_ref[...]
    product = jnp.sum(parts_ref[...], axis=0) + noise_var * direction
    product_ref[...] = product
    terms = jnp.concatenate(
        [direction * product, residual * residual, residual * product, product * product], axis=0
    )
    sums = jnp.sum(terms.T, axis=0, keepdims=True)
    row = jnp.concatenate([sums, jnp.zeros((1, LANES - sums.shape[1]), f32)], axis=1)
    stats_ref[...] = jnp.broadcast_to(row[None], stats_ref.shape)


def update_kernel(stats_ref, product_ref, dir_ref, res_ref, sol_ref, new_sol_ref, new_res_ref, new_dir_ref):
    sums = jnp.broadcast_to(jnp.sum(stats_ref[...], axis=0), (LANES, LANES)).T
    curvature, norm_old, cross, norm_product = (
        sums[k * PROBES : (k + 1) * PROBES] for k in range(4)
    )
    step_size = norm_old / curvature
    norm_new = norm_old + step_size * (step_size * norm_product - 2.0 * cross)
    direction = dir_ref[...]
    new_residual = res_ref[...] - step_size * product_ref[...]
    new_sol_ref[...] = sol_ref[...] + step_size * direction
    new_res_ref[...] = new_residual
    new_dir_ref[...] = new_residual + norm_new / norm_old * direction


def call(kernel, out_shape, n_in, scratch=(), limit=16, space=pltpu.VMEM):
    vmem = pl.BlockSpec(memory_space=pltpu.VMEM)
    many = isinstance(out_shape, (list, tuple))
    return pl.pallas_call(
        kernel,
        out_shape=out_shape,
        in_specs=[pl.BlockSpec(memory_space=space)] * n_in,
        out_specs=[vmem] * len(out_shape) if many else vmem,
        scratch_shapes=scratch,
        compiler_params=pltpu.CompilerParams(vmem_limit_bytes=limit * 2**20),
    )


def body(points, inv_scale, tasks, task_cov, solution, residual, direction):
    line, plane = SHAPE[0], math.prod(SHAPE[1:])
    dir_t, res_t, sol_t = direction.T, residual.T, solution.T
    row_send, col_send = call(
        pack_kernel,
        [
            jax.ShapeDtypeStruct((ROW_ROWS, LANES), bf16),
            jax.ShapeDtypeStruct((line, COL_ROWS, LANES), bf16),
        ],
        4,
        [
            pltpu.VMEM((FEATS, LANES), bf16),
            pltpu.VMEM((1, FEATS), f32),
            pltpu.VMEM((1, LANES), jnp.int32),
            pltpu.VMEM((PROBES, LANES), f32),
            pltpu.SemaphoreType.DMA((4,)),
        ],
        limit=60,
        space=pl.ANY,
    )(points.T, inv_scale[None, :], tasks[None, :], dir_t)
    cols = lax.all_to_all(col_send, LINE, 0, 0, axis_index_groups=GATHER_ORDER)
    rows = lax.all_gather(row_send, PLANE)
    partial = call(
        block_kernel,
        jax.ShapeDtypeStruct((plane, PROBES, LANES), f32),
        3,
        [
            pltpu.VMEM((DEPTH, plane * LANES), bf16),
            pltpu.VMEM((line * LANES, DEPTH), bf16),
            pltpu.VMEM((LEVELS * PROBES, line * LANES), bf16),
        ],
        limit=40,
    )(rows, cols, task_cov)
    parts = lax.all_to_all(partial, PLANE, 0, 0)
    product, stats = call(
        product_kernel,
        [
            jax.ShapeDtypeStruct((PROBES, LANES), f32),
            jax.ShapeDtypeStruct((plane, 1, LANES), f32),
        ],
        3,
    )(parts, dir_t, res_t)
    stats = jnp.sum(lax.all_to_all(stats, PLANE, 0, 0), axis=0)
    stats = jnp.broadcast_to(stats[None], (line,) + stats.shape)
    stats = lax.all_to_all(stats, LINE, 0, 0, axis_index_groups=SCALAR_ORDER)
    like = jax.ShapeDtypeStruct((PROBES, LANES), f32)
    new_solution, new_residual, new_direction = call(update_kernel, [like] * 3, 5)(
        stats, product, dir_t, res_t, sol_t
    )
    return (new_solution.T, new_residual.T, new_direction.T)


def solution(mesh):
    fine = Mesh(mesh.devices.reshape(SHAPE), AXES)
    rows, flat = P(AXES, None), P(AXES)
    return jax.shard_map(
        body,
        mesh=fine,
        in_specs=(rows, P(), flat, P(), rows, rows, rows),
        out_specs=(rows, rows, rows),
        check_vma=False,
    )
```

```python
import math

import jax
import jax.numpy as jnp
from jax import lax
from jax.experimental import pallas as pl
from jax.experimental.pallas import tpu as pltpu
from jax.sharding import Mesh
from jax.sharding import PartitionSpec as P

noise_var = 1.0
f32, bf16 = jnp.float32, jnp.bfloat16

FEATS, PROBES, LEVELS, LANES = 64, 16, 8, 128
DEPTH, COL_ROWS = FEATS + 16, FEATS + 8 + PROBES
ROW_TASK, COL_TASK, DIR_AT = 7, 0, FEATS + 8

SHAPE = (16, 4, 4, 2)
AXES = ("z", "x", "y", "core")
LINE, PLANE = "z", ("x", "y", "core")
GATHER_ORDER = [[(k + 12) % SHAPE[0] for k in range(SHAPE[0])]]
SCALAR_ORDER = [[(k + 8) % SHAPE[0] for k in range(SHAPE[0])]]


def split3(value):
    high = value.astype(bf16)
    rest = value - high.astype(f32)
    mid = rest.astype(bf16)
    return high, mid, (rest - mid.astype(f32)).astype(bf16)


def pack_kernel(points_in, scale_in, tasks_in, dir_in, rows_ref, cols_ref, points_ref, scale_ref, tasks_ref, dir_ref, sems):
    pairs = ((points_in, points_ref), (scale_in, scale_ref), (tasks_in, tasks_ref), (dir_in, dir_ref))
    copies = [pltpu.make_async_copy(src, dst, sems.at[k]) for k, (src, dst) in enumerate(pairs)]
    for copy in copies:
        copy.start()
    for copy in copies:
        copy.wait()
    scale = jnp.broadcast_to(scale_ref[...], (LANES, FEATS)).T
    scaled = (points_ref[...].astype(f32) * scale).astype(bf16)
    wide = scaled.astype(f32)
    parts = [p.astype(f32) for p in split3(jnp.sum(wide * wide, axis=0, keepdims=True) * -0.5)]
    task = tasks_ref[...].astype(f32)
    zero, one = jnp.zeros_like(task), jnp.ones_like(task)
    row_tail = jnp.concatenate([zero, one, one, one, *parts, task, jnp.zeros((8, LANES), f32)], axis=0)
    col_tail = jnp.concatenate([task, *parts, one, one, one, zero, dir_ref[...]], axis=0)
    rows_ref[...] = jnp.concatenate([scaled, row_tail.astype(bf16)], axis=0)
    whole = jnp.concatenate([scaled, col_tail.astype(bf16)], axis=0)
    for k in range(cols_ref.shape[0]):
        cols_ref[k] = whole


def block_kernel(rows_ref, cols_ref, cov_ref, out_ref, row_mat, col_mat, dir_mat):
    n_rows, n_cols = rows_ref.shape[0], cols_ref.shape[0]
    for k in range(n_rows):
        row_mat[:, k * LANES : (k + 1) * LANES] = rows_ref[k]
    for k in range(n_cols):
        at = pl.ds(k * LANES, LANES)
        col_mat[at, :] = cols_ref[k, :DEPTH, :].astype(f32).T.astype(bf16)
        task = cols_ref[k, FEATS:DIR_AT, :].astype(f32)[COL_TASK : COL_TASK + 1]
        dirs = cols_ref[k, DIR_AT:, :].astype(f32)
        dir_mat[:, at] = jnp.concatenate(
            [jnp.where(task == float(level), dirs, 0.0) for level in range(LEVELS)], axis=0
        ).astype(bf16)
    exponent = jnp.dot(col_mat[...], row_mat[...], preferred_element_type=f32)
    sums = jnp.dot(dir_mat[...], jnp.exp(exponent).astype(bf16), preferred_element_type=f32)
    for k in range(n_rows):
        task = rows_ref[k, FEATS:DEPTH, :].astype(f32)[ROW_TASK : ROW_TASK + 1]
        cov = jnp.zeros((LEVELS, LANES), f32)
        for level in range(LEVELS):
            cov = cov + jnp.where(task == float(level), cov_ref[:, level : level + 1], 0.0)
        total = jnp.zeros((PROBES, LANES), f32)
        for level in range(LEVELS):
            part = sums[level * PROBES : (level + 1) * PROBES, k * LANES : (k + 1) * LANES]
            total = total + cov[level : level + 1, :] * part
        out_ref[k] = total


def product_kernel(parts_ref, dir_ref, res_ref, product_ref, stats_ref):
    direction, residual = dir_ref[...], res_ref[...]
    product = jnp.sum(parts_ref[...], axis=0) + noise_var * direction
    product_ref[...] = product
    terms = jnp.concatenate(
        [direction * product, residual * residual, residual * product, product * product], axis=0
    )
    sums = jnp.sum(terms.T, axis=0, keepdims=True)
    row = jnp.concatenate([sums, jnp.zeros((1, LANES - sums.shape[1]), f32)], axis=1)
    stats_ref[...] = jnp.broadcast_to(row[None], stats_ref.shape)


def update_kernel(stats_ref, product_ref, dir_ref, res_ref, sol_ref, new_sol_ref, new_res_ref, new_dir_ref):
    sums = jnp.broadcast_to(jnp.sum(stats_ref[...], axis=0), (LANES, LANES)).T
    curvature, norm_old, cross, norm_product = (
        sums[k * PROBES : (k + 1) * PROBES] for k in range(4)
    )
    step_size = norm_old / curvature
    norm_new = norm_old + step_size * (step_size * norm_product - 2.0 * cross)
    direction = dir_ref[...]
    new_residual = res_ref[...] - step_size * product_ref[...]
    new_sol_ref[...] = sol_ref[...] + step_size * direction
    new_res_ref[...] = new_residual
    new_dir_ref[...] = new_residual + norm_new / norm_old * direction


def call(kernel, out_shape, n_in, scratch=(), limit=16, space=pltpu.VMEM):
    vmem = pl.BlockSpec(memory_space=pltpu.VMEM)
    many = isinstance(out_shape, (list, tuple))
    return pl.pallas_call(
        kernel,
        out_shape=out_shape,
        in_specs=[pl.BlockSpec(memory_space=space)] * n_in,
        out_specs=[vmem] * len(out_shape) if many else vmem,
        scratch_shapes=scratch,
        compiler_params=pltpu.CompilerParams(vmem_limit_bytes=limit * 2**20),
    )


def body(points, inv_scale, tasks, task_cov, solution, residual, direction):
    line, plane = SHAPE[0], math.prod(SHAPE[1:])
    dir_t, res_t, sol_t = direction.T, residual.T, solution.T
    row_send, col_send = call(
        pack_kernel,
        [
            jax.ShapeDtypeStruct((DEPTH, LANES), bf16),
            jax.ShapeDtypeStruct((line, COL_ROWS, LANES), bf16),
        ],
        4,
        [
            pltpu.VMEM((FEATS, LANES), bf16),
            pltpu.VMEM((1, FEATS), f32),
            pltpu.VMEM((1, LANES), jnp.int32),
            pltpu.VMEM((PROBES, LANES), f32),
            pltpu.SemaphoreType.DMA((4,)),
        ],
        limit=60,
        space=pl.ANY,
    )(points.T, inv_scale[None, :], tasks[None, :], dir_t)
    cols = lax.all_to_all(col_send, LINE, 0, 0, axis_index_groups=GATHER_ORDER)
    rows = lax.all_gather(row_send, PLANE)
    partial = call(
        block_kernel,
        jax.ShapeDtypeStruct((plane, PROBES, LANES), f32),
        3,
        [
            pltpu.VMEM((DEPTH, plane * LANES), bf16),
            pltpu.VMEM((line * LANES, DEPTH), bf16),
            pltpu.VMEM((LEVELS * PROBES, line * LANES), bf16),
        ],
        limit=36,
    )(rows, cols, task_cov)
    parts = lax.all_to_all(partial, PLANE, 0, 0)
    product, stats = call(
        product_kernel,
        [
            jax.ShapeDtypeStruct((PROBES, LANES), f32),
            jax.ShapeDtypeStruct((plane, 1, LANES), f32),
        ],
        3,
    )(parts, dir_t, res_t)
    stats = jnp.sum(lax.all_to_all(stats, PLANE, 0, 0), axis=0)
    stats = jnp.broadcast_to(stats[None], (line,) + stats.shape)
    stats = lax.all_to_all(stats, LINE, 0, 0, axis_index_groups=SCALAR_ORDER)
    like = jax.ShapeDtypeStruct((PROBES, LANES), f32)
    new_solution, new_residual, new_direction = call(update_kernel, [like] * 3, 5)(
        stats, product, dir_t, res_t, sol_t
    )
    return (new_solution.T, new_residual.T, new_direction.T)


def solution(mesh):
    fine = Mesh(mesh.devices.reshape(SHAPE), AXES)
    rows, flat = P(AXES, None), P(AXES)
    return jax.shard_map(
        body,
        mesh=fine,
        in_specs=(rows, P(), flat, P(), rows, rows, rows),
        out_specs=(rows, rows, rows),
        check_vma=False,
    )
```

```python
import math

import jax
import jax.numpy as jnp
from jax import lax
from jax.experimental import pallas as pl
from jax.experimental.pallas import tpu as pltpu
from jax.sharding import Mesh
from jax.sharding import PartitionSpec as P

noise_var = 1.0
f32, bf16 = jnp.float32, jnp.bfloat16

FEATS, PROBES, LEVELS, LANES = 64, 16, 8, 128
DEPTH, COL_ROWS = FEATS + 16, FEATS + 8 + PROBES
ROW_TASK, COL_TASK, DIR_AT = 7, 0, FEATS + 8

SHAPE = (16, 4, 4, 2)
AXES = ("z", "x", "y", "core")
LINE, PLANE = "z", ("x", "y", "core")
GATHER_ORDER = [[(k + 12) % SHAPE[0] for k in range(SHAPE[0])]]
SCALAR_ORDER = [[(k + 8) % SHAPE[0] for k in range(SHAPE[0])]]


def split3(value):
    high = value.astype(bf16)
    rest = value - high.astype(f32)
    mid = rest.astype(bf16)
    return high, mid, (rest - mid.astype(f32)).astype(bf16)


def pack_kernel(points_in, scale_in, tasks_in, dir_in, rows_ref, cols_ref, points_ref, scale_ref, tasks_ref, dir_ref, sems):
    pairs = ((points_in, points_ref), (scale_in, scale_ref), (tasks_in, tasks_ref), (dir_in, dir_ref))
    copies = [pltpu.make_async_copy(src, dst, sems.at[k]) for k, (src, dst) in enumerate(pairs)]
    for copy in copies:
        copy.start()
    for copy in copies:
        copy.wait()
    scale = jnp.broadcast_to(scale_ref[...], (LANES, FEATS)).T
    scaled = (points_ref[...].astype(f32) * scale).astype(bf16)
    wide = scaled.astype(f32)
    parts = [p.astype(f32) for p in split3(jnp.sum(wide * wide, axis=0, keepdims=True) * -0.5)]
    task = tasks_ref[...].astype(f32)
    zero, one = jnp.zeros_like(task), jnp.ones_like(task)
    row_tail = jnp.concatenate([zero, one, one, one, *parts, task, jnp.zeros((8, LANES), f32)], axis=0)
    col_tail = jnp.concatenate([task, *parts, one, one, one, zero, dir_ref[...]], axis=0)
    rows_ref[...] = jnp.concatenate([scaled, row_tail.astype(bf16)], axis=0)
    whole = jnp.concatenate([scaled, col_tail.astype(bf16)], axis=0)
    for k in range(cols_ref.shape[0]):
        cols_ref[k] = whole


def block_kernel(rows_ref, cols_ref, cov_ref, out_ref, row_mat, col_mat, dir_mat):
    n_rows, n_cols = rows_ref.shape[0], cols_ref.shape[0]
    for k in range(n_rows):
        row_mat[:, k * LANES : (k + 1) * LANES] = rows_ref[k]
    for k in range(n_cols):
        at = pl.ds(k * LANES, LANES)
        col_mat[at, :] = cols_ref[k, :DEPTH, :].T
        task = cols_ref[k, FEATS:DIR_AT, :].astype(f32)[COL_TASK : COL_TASK + 1]
        dirs = cols_ref[k, DIR_AT:, :].astype(f32)
        dir_mat[:, at] = jnp.concatenate(
            [jnp.where(task == float(level), dirs, 0.0) for level in range(LEVELS)], axis=0
        ).astype(bf16)
    exponent = jnp.dot(col_mat[...], row_mat[...], preferred_element_type=f32)
    sums = jnp.dot(dir_mat[...], jnp.exp(exponent).astype(bf16), preferred_element_type=f32)
    for k in range(n_rows):
        task = rows_ref[k, FEATS:DEPTH, :].astype(f32)[ROW_TASK : ROW_TASK + 1]
        cov = jnp.zeros((LEVELS, LANES), f32)
        for level in range(LEVELS):
            cov = cov + jnp.where(task == float(level), cov_ref[:, level : level + 1], 0.0)
        total = jnp.zeros((PROBES, LANES), f32)
        for level in range(LEVELS):
            part = sums[level * PROBES : (level + 1) * PROBES, k * LANES : (k + 1) * LANES]
            total = total + cov[level : level + 1, :] * part
        out_ref[k] = total


def product_kernel(parts_ref, dir_ref, res_ref, product_ref, stats_ref):
    direction, residual = dir_ref[...], res_ref[...]
    product = jnp.sum(parts_ref[...], axis=0) + noise_var * direction
    product_ref[...] = product
    terms = jnp.concatenate(
        [direction * product, residual * residual, residual * product, product * product], axis=0
    )
    sums = jnp.sum(terms.T, axis=0, keepdims=True)
    row = jnp.concatenate([sums, jnp.zeros((1, LANES - sums.shape[1]), f32)], axis=1)
    stats_ref[...] = jnp.broadcast_to(row[None], stats_ref.shape)


def update_kernel(stats_ref, product_ref, dir_ref, res_ref, sol_ref, new_sol_ref, new_res_ref, new_dir_ref):
    sums = jnp.broadcast_to(jnp.sum(stats_ref[...], axis=0), (LANES, LANES)).T
    curvature, norm_old, cross, norm_product = (
        sums[k * PROBES : (k + 1) * PROBES] for k in range(4)
    )
    step_size = norm_old / curvature
    norm_new = norm_old + step_size * (step_size * norm_product - 2.0 * cross)
    direction = dir_ref[...]
    new_residual = res_ref[...] - step_size * product_ref[...]
    new_sol_ref[...] = sol_ref[...] + step_size * direction
    new_res_ref[...] = new_residual
    new_dir_ref[...] = new_residual + norm_new / norm_old * direction


def call(kernel, out_shape, n_in, scratch=(), limit=16, space=pltpu.VMEM):
    vmem = pl.BlockSpec(memory_space=pltpu.VMEM)
    many = isinstance(out_shape, (list, tuple))
    return pl.pallas_call(
        kernel,
        out_shape=out_shape,
        in_specs=[pl.BlockSpec(memory_space=space)] * n_in,
        out_specs=[vmem] * len(out_shape) if many else vmem,
        scratch_shapes=scratch,
        compiler_params=pltpu.CompilerParams(vmem_limit_bytes=limit * 2**20),
    )


def body(points, inv_scale, tasks, task_cov, solution, residual, direction):
    line, plane = SHAPE[0], math.prod(SHAPE[1:])
    dir_t, res_t, sol_t = direction.T, residual.T, solution.T
    row_send, col_send = call(
        pack_kernel,
        [
            jax.ShapeDtypeStruct((DEPTH, LANES), bf16),
            jax.ShapeDtypeStruct((line, COL_ROWS, LANES), bf16),
        ],
        4,
        [
            pltpu.VMEM((FEATS, LANES), bf16),
            pltpu.VMEM((1, FEATS), f32),
            pltpu.VMEM((1, LANES), jnp.int32),
            pltpu.VMEM((PROBES, LANES), f32),
            pltpu.SemaphoreType.DMA((4,)),
        ],
        limit=60,
        space=pl.ANY,
    )(points.T, inv_scale[None, :], tasks[None, :], dir_t)
    cols = lax.all_to_all(col_send, LINE, 0, 0, axis_index_groups=GATHER_ORDER)
    rows = lax.all_gather(row_send, PLANE)
    partial = call(
        block_kernel,
        jax.ShapeDtypeStruct((plane, PROBES, LANES), f32),
        3,
        [
            pltpu.VMEM((DEPTH, plane * LANES), bf16),
            pltpu.VMEM((line * LANES, DEPTH), bf16),
            pltpu.VMEM((LEVELS * PROBES, line * LANES), bf16),
        ],
        limit=36,
    )(rows, cols, task_cov)
    parts = lax.all_to_all(partial, PLANE, 0, 0)
    product, stats = call(
        product_kernel,
        [
            jax.ShapeDtypeStruct((PROBES, LANES), f32),
            jax.ShapeDtypeStruct((plane, 1, LANES), f32),
        ],
        3,
    )(parts, dir_t, res_t)
    stats = jnp.sum(lax.all_to_all(stats, PLANE, 0, 0), axis=0)
    stats = jnp.broadcast_to(stats[None], (line,) + stats.shape)
    stats = lax.all_to_all(stats, LINE, 0, 0, axis_index_groups=SCALAR_ORDER)
    like = jax.ShapeDtypeStruct((PROBES, LANES), f32)
    new_solution, new_residual, new_direction = call(update_kernel, [like] * 3, 5)(
        stats, product, dir_t, res_t, sol_t
    )
    return (new_solution.T, new_residual.T, new_direction.T)


def solution(mesh):
    fine = Mesh(mesh.devices.reshape(SHAPE), AXES)
    rows, flat = P(AXES, None), P(AXES)
    return jax.shard_map(
        body,
        mesh=fine,
        in_specs=(rows, P(), flat, P(), rows, rows, rows),
        out_specs=(rows, rows, rows),
        check_vma=False,
    )
```
